32 devices in a mesh: parts: 2 (over x), tile: 8 (over z, y), stream: 2 (over core).
Axes of the slice: x: 2, y: 2, z: 4, core: 2. Of those that a mesh axis runs over, the one named last changes fastest.
Arguments:
- obs_rows: bfloat16 [131072, 128], P(('parts', 'tile', 'stream')), parts along dimension 0, may hold values from -6 to 6
- obs_instr: int32 [131072], P(('parts', 'tile', 'stream')), parts along dimension 0, may hold values from 0 to 3
- obs_target: int32 [131072, 1], P(('parts', 'tile', 'stream')), parts along dimension 0, may hold values from 0 to 15; in each aligned block of 4096 rows (0 to 4095, 4096 to 8191, ...) at most 512 rows name the same one
- obs_cell: int32 [131072], P(('parts', 'tile', 'stream')), parts along dimension 0, may hold values from 0 to 5759
- embed_weight: bfloat16 [8, 128, 256], P('stream'), may hold values from -0.5 to 0.5
- background: float32 [256], replicated, may hold values from -5 to 5
- stencil_taps: float32 [9, 256], replicated, may hold values from -2 to 2
- weight_in: bfloat16 [256, 1024], replicated, may hold values from -0.375 to 0.375
- weight_out: bfloat16 [1024, 256], replicated, may hold values from -0.1875 to 0.1875
- grid_cotangent: bfloat16 [128, 1440, 256], P(('parts', 'tile', 'stream')), parts along dimension 0, may hold values from -6 to 6
Outputs:
- grid_output: bfloat16 [128, 1440, 256], P(('parts', 'tile', 'stream')), parts along dimension 0
- embed_grad: float32 [16, 128, 256], P(('parts', 'stream')), parts along dimension 0
The draws below stay inside these ranges and needn't reach their ends.
There are 2 independent parts, one for each index of `parts`. The reference program is written for one: setup_inputs(seed, part) draws one part's arguments, and reference() takes and returns one part's arrays. A program takes and returns all parts, laid end to end along the dimension named above; an argument that names none is the same for every part. Nothing has to cross between parts.
Inputs may be any that keep to these rules, and one draw needn't show every extreme that they name: `obs_target`: among the 4096 observations of one device at most 512 name the same target.
All inputs are finite; a program needn't handle non-finite values.
Results may differ from the reference program's by a relative error of at most 0.015.
Values may be sent and summed in bfloat16 or wider, within the bound.
A program may use at most 192 MiB of HBM per device.

```python
import math
import jax
import jax.numpy as jnp
import numpy as np
from jax import lax

C = 256
F_OBS = 128
HID = 1024
LON = 1440
INS_DEV = 4
LAT_DEV = 4
OBS_DEV = 4096
PEERS = 16
INSTR = 8
CAPACITY = 512
OBS = 65536
GRID_LAT = 64
N_STREAM = 2


def place_ends(drawn, rng, least, high):
    longest = drawn.shape.index(max(drawn.shape))
    spots = []
    for shift in (0, 1):
        where = [jax.random.randint(jax.random.fold_in(rng, axis), (), 0, length) for axis, length in enumerate(drawn.shape)]
        where[longest] = (where[longest] + shift) % drawn.shape[longest]
        spots.append(tuple(where))
    return drawn.at[spots[0]].set(least).at[spots[1]].set(high)


def shard_levels(key, shape, pieces, low, top_value):
    level, own = 1.0, jax.random.fold_in(key, 6)
    for dim, shards_of in pieces:
        heights = jnp.exp(jax.random.uniform(jax.random.fold_in(own, dim), (shards_of,), jnp.float32, low / len(pieces), top_value / len(pieces)))
        level = level * jnp.repeat(heights, shape[dim] // shards_of).reshape([-1 if axis == dim else 1 for axis in range(len(shape))])
    return level


def assign_block(rng, own, number, rows, count, top, most, lean):
    sequence = jax.random.permutation(rng, count)
    heavy_load, ordinary = load_shares(count, rows * top, most, lean, True), load_shares(count, rows * top, most, lean, False)
    places = jnp.arange(count)

    def named(tallies, rotation):
        used = int((tallies > 0).sum())
        fixed = max(1, used // 4)
        shifted = fixed + (places - fixed + rotation * (used - fixed)) % max(1, count - fixed)
        return jnp.zeros((count,), jnp.int32).at[sequence[jnp.where(places < fixed, places, shifted)]].set(jnp.asarray(tallies, jnp.int32))

    tallies = jnp.where(number % 4 == 0, named(heavy_load, number // 4), named(ordinary, number - number // 4 - 1))
    mixed = jax.random.permutation(jax.random.fold_in(own, 3), count)
    source_of, taker = mixed[0:count // 2 * 2:2], mixed[1:count // 2 * 2:2]
    margin = jnp.minimum(tallies[source_of] - 1, most - tallies[taker]) // 2
    margin = jnp.where((source_of == sequence[0]) | (taker == sequence[0]) | (tallies[taker] == 0), 0, jnp.maximum(margin, 0))
    shifted = jax.random.randint(jax.random.fold_in(own, 4), (count // 2,), 0, 1 << 20) % (margin + 1)
    tallies = tallies.at[source_of].add(-shifted).at[taker].add(shifted)
    items = jnp.searchsorted(jnp.cumsum(tallies), jnp.arange(rows * top), side="right").astype(jnp.int32)
    grid = items.reshape(top, rows).T
    grid = grid[jax.random.permutation(jax.random.fold_in(own, 1), rows)]
    rotation = jax.random.randint(jax.random.fold_in(own, 2), (rows, 1), 0, top)
    return jnp.take_along_axis(grid, (jnp.arange(top)[None, :] + rotation) % top, axis=1)


def load_shares(number_of, total, limit, lean, full):
    loads = [(1 << 20) // math.isqrt(grade ** lean) + 1 for grade in range(1, number_of + 1)]
    largest = limit if full else min(limit, max(-(-total // number_of), total * loads[0] // sum(loads)))
    least = 1 if total - largest >= number_of - 1 else 0
    holding, surplus = [largest] + [least] * (number_of - 1), total - largest - least * (number_of - 1)
    while surplus > 0:
        candidates = [i for i in range(1, number_of) if holding[i] < largest] or [i for i in range(1, number_of) if holding[i] < limit]
        mass, remaining = sum([loads[i] for i in candidates]), surplus
        for i in candidates:
            addition = min(limit - holding[i], max(1, remaining * loads[i] // mass), surplus)
            holding[i] = holding[i] + addition
            surplus = surplus - addition
    return np.array(holding)


def bell_draw(rng, extent, width, limit, split=(), kind=jnp.bfloat16):
    drawn = width * jax.random.normal(rng, extent, jnp.float32)
    if split:
        drawn = drawn * shard_levels(rng, extent, split, -0.22, 0.18)
    return jnp.clip(drawn, -limit, limit).astype(kind)


def setup_inputs(seed: int = 0, part: int = 0) -> dict:
    seeds = jax.random.split(jax.random.key(seed), 11)
    part_splits = jax.random.split(jax.random.fold_in(seeds[10], part), 11)
    obs_rows = bell_draw(part_splits[0], (OBS, F_OBS), 1.0, 6.0, ((0, 16),))
    obs_instr = place_ends(jax.random.randint(part_splits[1], (OBS,), 0, INS_DEV), jax.random.fold_in(part_splits[1], 1), 0, INS_DEV - 1).astype(jnp.int32)
    obs_target_keys = jax.random.split(jax.random.fold_in(part_splits[2], 1), OBS // OBS_DEV)
    obs_target_turns = jax.random.permutation(jax.random.fold_in(part_splits[2], 3), OBS // OBS_DEV)
    obs_target = jax.vmap(lambda own, number: assign_block(jax.random.fold_in(part_splits[2], 2), own, number, OBS_DEV, PEERS, 1, CAPACITY, 2))(obs_target_keys, obs_target_turns).reshape((OBS, 1))
    obs_cell = place_ends(jax.random.randint(part_splits[3], (OBS,), 0, LAT_DEV * LON), jax.random.fold_in(part_splits[3], 1), 0, (LAT_DEV * LON) - 1).astype(jnp.int32)
    embed_weight = bell_draw(seeds[4], (INSTR, F_OBS, C), F_OBS ** -0.5, 0.5, ((0, 2),))
    background = bell_draw(seeds[5], (C,), 1.0, 5.0, (), jnp.float32)
    stencil_taps = bell_draw(seeds[6], (9, C), 0.35, 2.0, (), jnp.float32)
    weight_in = bell_draw(seeds[7], (C, HID), C ** -0.5, 0.375)
    weight_out = bell_draw(seeds[8], (HID, C), HID ** -0.5, 0.1875)
    grid_cotangent = bell_draw(part_splits[9], (GRID_LAT, LON, C), 1.0, 6.0, ((0, 16),))
    return {"obs_rows": obs_rows, "obs_instr": obs_instr, "obs_target": obs_target, "obs_cell": obs_cell, "embed_weight": embed_weight, "background": background, "stencil_taps": stencil_taps, "weight_in": weight_in, "weight_out": weight_out, "grid_cotangent": grid_cotangent}


def embed(obs_rows, instrument, weights):

    def one(current, entry_pair):
        number, matrix = entry_pair
        product = jnp.dot(obs_rows, matrix, preferred_element_type=jnp.float32)
        return (jnp.where((instrument == number)[:, None], product, current), None)
    initial = jnp.zeros((obs_rows.shape[0], weights.shape[2]), jnp.float32)
    result, _ = lax.scan(one, initial, (jnp.arange(weights.shape[0], dtype=jnp.int32), weights))
    return result.astype(jnp.bfloat16)

def stencil(padded, stencil_taps, orient):
    row_count = padded.shape[0] - 2
    field = padded.astype(jnp.float32)
    summed = jnp.zeros((row_count,) + padded.shape[1:], jnp.float32)
    for row_step in range(3):
        for col_step in range(3):
            offset = 1 + orient * (row_step - 1)
            window = lax.slice_in_dim(field, offset, offset + row_count, axis=0)
            window = jnp.roll(window, -orient * (col_step - 1), axis=1)
            summed = summed + stencil_taps[row_step * 3 + col_step] * window
    return summed

def branch(mixed, weight_in, weight_out):
    inverse_rms = lax.rsqrt(lax.optimization_barrier(jnp.mean(mixed * mixed, axis=-1, keepdims=True)) + 1e-06)
    normed = (mixed * inverse_rms).astype(jnp.bfloat16)
    hidden = jax.nn.gelu(jnp.dot(normed, weight_in, preferred_element_type=jnp.float32), approximate=True).astype(jnp.bfloat16)
    return jnp.dot(hidden, weight_out, preferred_element_type=jnp.float32)

def layer_both(mixed, cotangent, weight_in, weight_out):
    result, pull = jax.vjp(lambda inner: branch(inner, weight_in, weight_out), mixed)
    grad_mixed = pull(cotangent.astype(jnp.float32))[0].astype(jnp.bfloat16)
    return (result, grad_mixed)

def reference(obs_rows, obs_instr, obs_target, obs_cell, embed_weight, background, stencil_taps, weight_in, weight_out, grid_cotangent):
    row_ids = jnp.arange(OBS, dtype=jnp.int32)
    stream_ids = row_ids // OBS_DEV % N_STREAM
    instrument = stream_ids * INS_DEV + obs_instr
    emb = embed(obs_rows, instrument, embed_weight)
    band_cells = LAT_DEV * LON
    all_cells = GRID_LAT * LON
    global_cell = obs_target[:, 0] * band_cells + obs_cell
    deposit = jnp.zeros((all_cells, C), jnp.float32).at[global_cell].add(emb.astype(jnp.float32))
    arrivals = jnp.zeros((all_cells,), jnp.float32).at[global_cell].add(1.0)
    field = ((deposit + background[None, :]) / (1.0 + arrivals)[:, None]).astype(jnp.bfloat16)
    field = field.reshape(GRID_LAT, LON, C)
    padded = jnp.pad(field, ((1, 1), (0, 0), (0, 0)))
    mixed = stencil(padded, stencil_taps, 1)
    bands = GRID_LAT // LAT_DEV
    mixed_blocks = mixed.reshape(bands, band_cells, C)
    cot_blocks = grid_cotangent.reshape(bands, band_cells, C)
    results, grads = lax.map(lambda pair: layer_both(pair[0], pair[1], weight_in, weight_out), (mixed_blocks, cot_blocks))
    grid_output = (field.astype(jnp.float32) + results.reshape(GRID_LAT, LON, C)).astype(jnp.bfloat16)
    grad_mixed = grads.reshape(GRID_LAT, LON, C)
    padded_grad = jnp.pad(grad_mixed, ((1, 1), (0, 0), (0, 0)))
    grad_field = grid_cotangent.astype(jnp.float32) + stencil(padded_grad, stencil_taps, -1)
    grad_cells = grad_field.reshape(all_cells, C) / (1.0 + arrivals)[:, None]
    grad_emb = grad_cells[global_cell].astype(jnp.bfloat16)

    def one_instrument(number):
        masked = jnp.where((instrument == number)[:, None], grad_emb, jnp.zeros_like(grad_emb))
        return jnp.dot(obs_rows.T, masked, preferred_element_type=jnp.float32)
    embed_grad = lax.map(one_instrument, jnp.arange(INSTR, dtype=jnp.int32))
    return (grid_output, embed_grad)
```

```python
import functools

import jax
import jax.numpy as jnp
from jax import lax
from jax.experimental import pallas as pl
from jax.experimental.pallas import tpu as pltpu
from jax.sharding import PartitionSpec as P


def padded_2(block, sides, width):
    for axis, dim in sides:
        count = lax.axis_size(axis)
        forward = [(i, i + 1) for i in range(count - 1)]
        backward = [(target, source) for source, target in forward]
        low = lax.ppermute(
            lax.slice_in_dim(block, block.shape[dim] - width, None, axis=dim), axis, forward
        )
        high = lax.ppermute(lax.slice_in_dim(block, 0, width, axis=dim), axis, backward)
        block = jnp.concatenate([low, block, high], axis=dim)
    return block


def pack_kernel(slot_ref, code_ref, rows_ref, out_rows, out_codes, rows_wide, packed):
    rows = rows_ref.shape[0]
    slots = out_rows.shape[0]
    step = 256

    @pl.loop(0, rows // step)
    def _(block):
        at = pl.ds(pl.multiple_of(block * step, step), step)
        rows_wide[at, :] = rows_ref[at, :].astype(jnp.float32)

    @pl.loop(0, slots // step)
    def _(block):
        at = pl.ds(pl.multiple_of(block * step, step), step)
        packed[at, :] = jnp.zeros((step, packed.shape[1]), jnp.float32)

    group = 16

    @pl.loop(0, rows // group)
    def _(block):
        base = block * group
        for inner in range(group):
            slot = slot_ref[base + inner]
            packed[pl.ds(slot, 1), :] = rows_wide[pl.ds(base + inner, 1), :]
            out_codes[slot] = code_ref[base + inner]

    @pl.loop(0, slots // step)
    def _(block):
        at = pl.ds(pl.multiple_of(block * step, step), step)
        out_rows[at, :] = packed[at, :].astype(jnp.bfloat16)


def pack(slot_index, codes, rows, slot_total):
    count, features = rows.shape
    smem = pl.BlockSpec(memory_space=pltpu.SMEM)
    vmem = pl.BlockSpec(memory_space=pltpu.VMEM)
    return pl.pallas_call(
        pack_kernel,
        out_shape=(
            jax.ShapeDtypeStruct((slot_total, features), jnp.bfloat16),
            jax.ShapeDtypeStruct((slot_total,), jnp.int32),
        ),
        in_specs=[smem, smem, vmem],
        out_specs=(vmem, smem),
        scratch_shapes=[
            pltpu.VMEM((count, features), jnp.float32),
            pltpu.VMEM((slot_total, features), jnp.float32),
        ],
        compiler_params=pltpu.CompilerParams(vmem_limit_bytes=24 << 20),
    )(slot_index, codes, rows)


def deposit_kernel(
    instr_dev,
    capacity,
    code_ref,
    cell_ref,
    bound_ref,
    rows_ref,
    weight_ref,
    background_ref,
    sums_out,
    field_out,
    density_out,
    even_sums,
    odd_sums,
    even_count,
    odd_count,
    even_rows,
    odd_rows,
):
    cells = field_out.shape[0]
    features = rows_ref.shape[1]
    pairs = rows_ref.shape[0] // (2 * capacity)
    step = 480

    @pl.loop(0, instr_dev * cells // step)
    def _(block):
        at = pl.ds(pl.multiple_of(block * step, 32), step)
        even_sums[at, :] = jnp.zeros((step, features), jnp.float32)
        odd_sums[at, :] = jnp.zeros((step, features), jnp.float32)

    @pl.loop(0, cells // step)
    def _(block):
        at = pl.ds(pl.multiple_of(block * step, 32), step)
        even_count[at, :] = jnp.zeros((step, features), jnp.float32)
        odd_count[at, :] = jnp.zeros((step, features), jnp.float32)

    one = jnp.ones((1, features), jnp.float32)
    group = 8

    @pl.loop(0, pairs)
    def _(pair):
        first = pl.multiple_of(pair * 2 * capacity, capacity)
        second = pl.multiple_of(first + capacity, capacity)
        even_rows[...] = rows_ref[pl.ds(first, capacity), :].astype(jnp.float32)
        odd_rows[...] = rows_ref[pl.ds(second, capacity), :].astype(jnp.float32)

        @pl.loop(0, bound_ref[pair])
        def _(block):
            base = block * group
            for inner in range(group):
                place = base + inner
                even_code = code_ref[first + place]
                odd_code = code_ref[second + place]
                even_cell = cell_ref[first + place]
                odd_cell = cell_ref[second + place]
                even_sums[pl.ds(even_code, 1), :] += even_rows[pl.ds(place, 1), :]
                odd_sums[pl.ds(odd_code, 1), :] += odd_rows[pl.ds(place, 1), :]
                even_count[pl.ds(even_cell, 1), :] += one
                odd_count[pl.ds(odd_cell, 1), :] += one

    @pl.loop(0, cells // step)
    def _(block):
        start = pl.multiple_of(block * step, 32)
        at = pl.ds(start, step)
        pieces = []
        for sums in (even_sums, odd_sums):
            for number in range(instr_dev):
                piece = sums[pl.ds(number * cells + start, step), :]
                pieces.append(piece.astype(jnp.bfloat16))
        wide = jnp.concatenate(pieces, axis=1)
        sums_out[at, :] = wide
        deposit = jnp.dot(wide, weight_ref[...], preferred_element_type=jnp.float32)
        density = 1.0 + (even_count[at, :] + odd_count[at, :])
        density_out[at, :] = density
        density = jnp.concatenate([density] * (deposit.shape[1] // features), axis=1)
        field_out[at, :] = ((deposit + background_ref[...]) / density).astype(jnp.bfloat16)


def deposit_cells(codes, cells, bounds, rows, weights, background, instr_dev, band_cells, capacity):
    features = rows.shape[1]
    width = weights.shape[1]
    smem = pl.BlockSpec(memory_space=pltpu.SMEM)
    vmem = pl.BlockSpec(memory_space=pltpu.VMEM)
    sums = pltpu.VMEM((instr_dev * band_cells + 8, features), jnp.float32)
    counts = pltpu.VMEM((band_cells + 8, features), jnp.float32)
    held = pltpu.VMEM((capacity, features), jnp.float32)
    return pl.pallas_call(
        functools.partial(deposit_kernel, instr_dev, capacity),
        out_shape=(
            jax.ShapeDtypeStruct((band_cells, weights.shape[0]), jnp.bfloat16),
            jax.ShapeDtypeStruct((band_cells, width), jnp.bfloat16),
            jax.ShapeDtypeStruct((band_cells, features), jnp.float32),
        ),
        in_specs=[smem, smem, smem, vmem, vmem, vmem],
        out_specs=(vmem, vmem, vmem),
        scratch_shapes=[sums, sums, counts, counts, held, held],
        compiler_params=pltpu.CompilerParams(vmem_limit_bytes=58 << 20),
    )(codes, cells, bounds, rows, weights, background.reshape(1, width))


def sum_over_tile(value):
    count = lax.axis_size("tile")
    if count & (count - 1):
        return lax.psum(value.astype(jnp.bfloat16), "tile").astype(jnp.float32)
    distance = 1
    while distance < count:
        mine = value.astype(jnp.bfloat16)
        other = lax.ppermute(mine, "tile", [(i, i ^ distance) for i in range(count)])
        value = mine.astype(jnp.float32) + other.astype(jnp.float32)
        distance *= 2
    return value


def stencil(padded, stencil_taps, orient):
    row_count = padded.shape[0] - 2
    field = padded.astype(jnp.float32)
    summed = jnp.zeros((row_count,) + padded.shape[1:], jnp.float32)
    for row_step in range(3):
        for col_step in range(3):
            offset = 1 + orient * (row_step - 1)
            window = lax.slice_in_dim(field, offset, offset + row_count, axis=0)
            window = jnp.roll(window, -orient * (col_step - 1), axis=1)
            summed = summed + stencil_taps[row_step * 3 + col_step] * window
    return summed


def branch(mixed, weight_in, weight_out):
    inverse_rms = lax.rsqrt(jnp.mean(mixed * mixed, axis=-1, keepdims=True) + 1e-06)
    normed = (mixed * inverse_rms).astype(jnp.bfloat16)
    hidden = jax.nn.gelu(
        jnp.dot(normed, weight_in, preferred_element_type=jnp.float32), approximate=True
    ).astype(jnp.bfloat16)
    return jnp.dot(hidden, weight_out, preferred_element_type=jnp.float32)


def on_device(
    obs_rows,
    obs_instr,
    obs_target,
    obs_cell,
    embed_weight,
    background,
    stencil_taps,
    weight_in,
    weight_out,
    grid_cotangent,
):
    peer_count = lax.axis_size(("tile", "stream"))
    stream = lax.axis_index("stream")
    swap = [(0, 1), (1, 0)]
    rows_dev, features = obs_rows.shape
    instr_dev = embed_weight.shape[0]
    capacity = 2 * rows_dev // peer_count
    lat_rows, lon_cells, width = grid_cotangent.shape
    band_cells = lat_rows * lon_cells
    other_weight = lax.ppermute(embed_weight, "stream", swap)
    weights = jnp.where(
        stream == 0,
        jnp.concatenate([embed_weight, other_weight], axis=0),
        jnp.concatenate([other_weight, embed_weight], axis=0),
    ).reshape(2 * instr_dev * features, width)
    destination = obs_target[:, 0]
    onehot = (destination[:, None] == jnp.arange(peer_count, dtype=jnp.int32)[None, :]).astype(
        jnp.int32
    )
    running = jnp.cumsum(onehot, axis=0)
    totals = running[-1]
    position = jnp.sum((running - onehot) * onehot, axis=1)
    slot_index = destination * capacity + position
    slot_total = peer_count * capacity
    spare = instr_dev * band_cells
    send_rows, send_codes = pack(
        slot_index, obs_instr * band_cells + obs_cell, obs_rows, slot_total
    )
    send_codes = jnp.where(
        jnp.arange(capacity, dtype=jnp.int32)[None, :] < totals[:, None],
        send_codes.reshape(peer_count, capacity),
        spare,
    )
    exchange = functools.partial(
        lax.all_to_all, axis_name=("tile", "stream"), split_axis=0, concat_axis=0, tiled=True
    )
    recv_codes = exchange(send_codes)
    recv_rows = exchange(send_rows.reshape(peer_count, capacity, features))
    held = jnp.sum((recv_codes < spare).astype(jnp.int32), axis=1)
    bounds = (jnp.max(held.reshape(-1, 2), axis=1) + 7) // 8
    recv_cells = jnp.where(recv_codes < spare, recv_codes % band_cells, band_cells)
    sums, field, density = deposit_cells(
        recv_codes.reshape(slot_total),
        recv_cells.reshape(slot_total),
        bounds,
        recv_rows.reshape(slot_total, features),
        weights,
        background,
        instr_dev,
        band_cells,
        capacity,
    )
    field = field.reshape(lat_rows, lon_cells, width)
    padded = padded_2(field, ((("tile", "stream"), 0),), 1)
    mixed = stencil(padded, stencil_taps, 1).reshape(band_cells, width)
    result, pull = jax.vjp(lambda inner: branch(inner, weight_in, weight_out), mixed)
    grid_output = (field.astype(jnp.float32) + result.reshape(lat_rows, lon_cells, width)).astype(
        jnp.bfloat16
    )
    grad_mixed = pull(grid_cotangent.reshape(band_cells, width).astype(jnp.float32))[0].astype(
        jnp.bfloat16
    )
    padded_grad = padded_2(
        grad_mixed.reshape(lat_rows, lon_cells, width), ((("tile", "stream"), 0),), 1
    )
    grad_field = grid_cotangent.astype(jnp.float32) + stencil(padded_grad, stencil_taps, -1)
    grad_cells = grad_field.reshape(band_cells, width) / density[:, :1]
    local_grad = lax.dot_general(
        sums,
        grad_cells.astype(jnp.bfloat16),
        (((0,), (0,)), ((), ())),
        preferred_element_type=jnp.float32,
    ).reshape(2, instr_dev, features, width)
    keep = jnp.where(stream == 0, local_grad[0], local_grad[1])
    give = jnp.where(stream == 0, local_grad[1], local_grad[0]).astype(jnp.bfloat16)
    group_grad = keep + lax.ppermute(give, "stream", swap).astype(jnp.float32)
    return (grid_output, sum_over_tile(group_grad))


def solution(mesh):
    in_specs = (
        P(("parts", "tile", "stream"), None),
        P(("parts", "tile", "stream")),
        P(("parts", "tile", "stream"), None),
        P(("parts", "tile", "stream")),
        P("stream", None, None),
        P(),
        P(),
        P(),
        P(),
        P(("parts", "tile", "stream"), None, None),
    )
    out_specs = (P(("parts", "tile", "stream"), None, None), P(("parts", "stream"), None, None))
    return jax.shard_map(
        on_device, mesh=mesh, in_specs=in_specs, out_specs=out_specs, check_vma=False
    )
```

```python
import functools

import jax
import jax.numpy as jnp
from jax import lax
from jax.experimental import pallas as pl
from jax.experimental.pallas import tpu as pltpu
from jax.sharding import PartitionSpec as P


def edge_rows(block):
    axes = ("tile", "stream")
    count = lax.axis_size(axes)
    forward = [(i, i + 1) for i in range(count - 1)]
    backward = [(target, source) for source, target in forward]
    return lax.ppermute(block[-1:], axes, forward), lax.ppermute(block[:1], axes, backward)


def pack_kernel(slot_ref, code_ref, rows_ref, out_rows, out_codes, rows_wide, packed):
    rows = rows_ref.shape[0]
    slots = out_rows.shape[0]
    step = 256

    @pl.loop(0, rows // step)
    def _(block):
        at = pl.ds(pl.multiple_of(block * step, step), step)
        rows_wide[at, :] = rows_ref[at, :].astype(jnp.float32)

    @pl.loop(0, slots // step)
    def _(block):
        at = pl.ds(pl.multiple_of(block * step, step), step)
        packed[at, :] = jnp.zeros((step, packed.shape[1]), jnp.float32)

    group = 16

    @pl.loop(0, rows // group)
    def _(block):
        base = block * group
        for inner in range(group):
            slot = slot_ref[base + inner]
            packed[pl.ds(slot, 1), :] = rows_wide[pl.ds(base + inner, 1), :]
            out_codes[slot] = code_ref[base + inner]

    @pl.loop(0, slots // step)
    def _(block):
        at = pl.ds(pl.multiple_of(block * step, step), step)
        out_rows[at, :] = packed[at, :].astype(jnp.bfloat16)


def pack(slot_index, codes, rows, slot_total):
    count, features = rows.shape
    smem = pl.BlockSpec(memory_space=pltpu.SMEM)
    vmem = pl.BlockSpec(memory_space=pltpu.VMEM)
    return pl.pallas_call(
        pack_kernel,
        out_shape=(
            jax.ShapeDtypeStruct((slot_total, features), jnp.bfloat16),
            jax.ShapeDtypeStruct((slot_total,), jnp.int32),
        ),
        in_specs=[smem, smem, vmem],
        out_specs=(vmem, smem),
        scratch_shapes=[
            pltpu.VMEM((count, features), jnp.float32),
            pltpu.VMEM((slot_total, features), jnp.float32),
        ],
        compiler_params=pltpu.CompilerParams(vmem_limit_bytes=24 << 20),
    )(slot_index, codes, rows)


def deposit_kernel(
    instr_dev,
    capacity,
    code_ref,
    cell_ref,
    bound_ref,
    rows_ref,
    weight_ref,
    background_ref,
    sums_out,
    field_out,
    density_out,
    even_sums,
    odd_sums,
    even_count,
    odd_count,
    even_rows,
    odd_rows,
):
    cells = field_out.shape[0]
    features = rows_ref.shape[1]
    pairs = rows_ref.shape[0] // (2 * capacity)
    step = 480

    @pl.loop(0, instr_dev * cells // step)
    def _(block):
        at = pl.ds(pl.multiple_of(block * step, 32), step)
        even_sums[at, :] = jnp.zeros((step, features), jnp.float32)
        odd_sums[at, :] = jnp.zeros((step, features), jnp.float32)

    @pl.loop(0, cells // step)
    def _(block):
        at = pl.ds(pl.multiple_of(block * step, 32), step)
        even_count[at, :] = jnp.zeros((step, features), jnp.float32)
        odd_count[at, :] = jnp.zeros((step, features), jnp.float32)

    one = jnp.ones((1, features), jnp.float32)
    group = 8

    @pl.loop(0, pairs)
    def _(pair):
        first = pl.multiple_of(pair * 2 * capacity, capacity)
        second = pl.multiple_of(first + capacity, capacity)
        even_rows[...] = rows_ref[pl.ds(first, capacity), :].astype(jnp.float32)
        odd_rows[...] = rows_ref[pl.ds(second, capacity), :].astype(jnp.float32)

        @pl.loop(0, bound_ref[pair])
        def _(block):
            base = block * group
            for inner in range(group):
                place = base + inner
                even_code = code_ref[first + place]
                odd_code = code_ref[second + place]
                even_cell = cell_ref[first + place]
                odd_cell = cell_ref[second + place]
                even_sums[pl.ds(even_code, 1), :] += even_rows[pl.ds(place, 1), :]
                odd_sums[pl.ds(odd_code, 1), :] += odd_rows[pl.ds(place, 1), :]
                even_count[pl.ds(even_cell, 1), :] += one
                odd_count[pl.ds(odd_cell, 1), :] += one

    @pl.loop(0, cells // step)
    def _(block):
        start = pl.multiple_of(block * step, 32)
        at = pl.ds(start, step)
        pieces = []
        for sums in (even_sums, odd_sums):
            for number in range(instr_dev):
                piece = sums[pl.ds(number * cells + start, step), :]
                pieces.append(piece.astype(jnp.bfloat16))
        wide = jnp.concatenate(pieces, axis=1)
        sums_out[at, :] = wide
        deposit = jnp.dot(wide, weight_ref[...], preferred_element_type=jnp.float32)
        density = 1.0 + (even_count[at, :] + odd_count[at, :])
        density_out[at, :] = density
        density = jnp.concatenate([density] * (deposit.shape[1] // features), axis=1)
        field_out[at, :] = ((deposit + background_ref[...]) / density).astype(jnp.bfloat16)


def deposit_cells(codes, cells, bounds, rows, weights, background, instr_dev, band_cells, capacity):
    features = rows.shape[1]
    width = weights.shape[1]
    smem = pl.BlockSpec(memory_space=pltpu.SMEM)
    vmem = pl.BlockSpec(memory_space=pltpu.VMEM)
    sums = pltpu.VMEM((instr_dev * band_cells + 8, features), jnp.float32)
    counts = pltpu.VMEM((band_cells + 8, features), jnp.float32)
    held = pltpu.VMEM((capacity, features), jnp.float32)
    return pl.pallas_call(
        functools.partial(deposit_kernel, instr_dev, capacity),
        out_shape=(
            jax.ShapeDtypeStruct((band_cells, weights.shape[0]), jnp.bfloat16),
            jax.ShapeDtypeStruct((band_cells, width), jnp.bfloat16),
            jax.ShapeDtypeStruct((band_cells, features), jnp.float32),
        ),
        in_specs=[smem, smem, smem, vmem, vmem, vmem],
        out_specs=(vmem, vmem, vmem),
        scratch_shapes=[sums, sums, counts, counts, held, held],
        compiler_params=pltpu.CompilerParams(vmem_limit_bytes=58 << 20),
    )(codes, cells, bounds, rows, weights, background.reshape(1, width))


def sum_over_tile(value):
    count = lax.axis_size("tile")
    if count & (count - 1):
        return lax.psum(value.astype(jnp.bfloat16), "tile").astype(jnp.float32)
    distance = 1
    while distance < count:
        mine = value.astype(jnp.bfloat16)
        other = lax.ppermute(mine, "tile", [(i, i ^ distance) for i in range(count)])
        value = mine.astype(jnp.float32) + other.astype(jnp.float32)
        distance *= 2
    return value


HALO = 16
CHUNK = 288


def fill_padded(padded, low_ref, block_ref, high_ref):
    rows, columns = block_ref.shape[0], block_ref.shape[1]
    for row in range(rows + 2):
        if row == 0:
            source, at = low_ref, 0
        elif row == rows + 1:
            source, at = high_ref, 0
        else:
            source, at = block_ref, row - 1
        padded[row, HALO : HALO + columns, :] = source[at]
        padded[row, 0:HALO, :] = source[at, columns - HALO : columns, :]
        padded[row, HALO + columns : 2 * HALO + columns, :] = source[at, 0:HALO, :]


def stencil(padded, taps_ref, row, start, orient):
    size = CHUNK + 2 * HALO
    rows = [
        padded[row + step, pl.ds(start, size), :].astype(jnp.float32) for step in range(3)
    ]
    total = None
    for col_step in range(3):
        summed = None
        for row_step in range(3):
            tap = taps_ref[pl.ds(row_step * 3 + col_step, 1), :]
            term = tap * rows[1 + orient * (row_step - 1)]
            summed = term if summed is None else summed + term
        shift = -orient * (col_step - 1)
        if shift:
            summed = pltpu.roll(summed, shift % size, 0)
        summed = summed[HALO : HALO + CHUNK]
        total = summed if total is None else total + summed
    return total


def layer_kernel(
    low_ref,
    field_ref,
    high_ref,
    taps_ref,
    in_ref,
    out_ref,
    in_t_ref,
    out_t_ref,
    cot_ref,
    grid_ref,
    grad_ref,
    padded,
):
    fill_padded(padded, low_ref, field_ref, high_ref)
    rows, columns = field_ref.shape[0], field_ref.shape[1]
    pieces = columns // CHUNK

    @pl.loop(0, rows * pieces)
    def _(index):
        row = index // pieces
        start = pl.multiple_of((index % pieces) * CHUNK, 32)
        at = pl.ds(start, CHUNK)
        mixed = stencil(padded, taps_ref, row, start, 1)
        inverse = lax.rsqrt(jnp.mean(mixed * mixed, axis=1, keepdims=True) + 1e-06)
        normed = (mixed * inverse).astype(jnp.bfloat16)
        inner = jnp.dot(normed, in_ref[...], preferred_element_type=jnp.float32)
        cot = cot_ref[row, at, :]
        grad_hidden = jnp.dot(cot, out_t_ref[...], preferred_element_type=jnp.float32)
        grad_hidden = grad_hidden.astype(jnp.bfloat16).astype(jnp.float32)
        scale = 0.7978845608028654
        square = inner * inner
        bent = jnp.tanh(inner * (scale + (scale * 0.044715) * square))
        half = 0.5 + 0.5 * bent
        hidden = (inner * half).astype(jnp.bfloat16)
        slope = (2.0 * scale) + (6.0 * scale * 0.044715) * square
        grad_inner = grad_hidden * (half + inner * (half - half * half) * slope)
        result = jnp.dot(hidden, out_ref[...], preferred_element_type=jnp.float32)
        grid_ref[row, at, :] = (field_ref[row, at, :].astype(jnp.float32) + result).astype(
            jnp.bfloat16
        )
        grad_normed = jnp.dot(
            grad_inner.astype(jnp.bfloat16), in_t_ref[...], preferred_element_type=jnp.float32
        )
        grad_normed = grad_normed.astype(jnp.bfloat16).astype(jnp.float32)
        along = jnp.mean(mixed * grad_normed, axis=1, keepdims=True)
        grad_mixed = inverse * grad_normed - mixed * (along * (inverse * inverse * inverse))
        grad_ref[row, at, :] = grad_mixed.astype(jnp.bfloat16)


def layer(edges, field, taps, weight_in, weight_out, cotangent):
    rows, columns, width = field.shape
    vmem = pl.BlockSpec(memory_space=pltpu.VMEM)
    shape = jax.ShapeDtypeStruct(field.shape, jnp.bfloat16)
    return pl.pallas_call(
        layer_kernel,
        out_shape=(shape, shape),
        in_specs=[vmem] * 9,
        out_specs=(vmem, vmem),
        scratch_shapes=[pltpu.VMEM((rows + 2, columns + 2 * HALO, width), jnp.bfloat16)],
        compiler_params=pltpu.CompilerParams(vmem_limit_bytes=40 << 20),
    )(edges[0], field, edges[1], taps, weight_in, weight_out, weight_in.T, weight_out.T, cotangent)


def back_kernel(low_ref, grad_ref, high_ref, taps_ref, cot_ref, density_ref, cells_ref, padded):
    fill_padded(padded, low_ref, grad_ref, high_ref)
    rows, columns = grad_ref.shape[0], grad_ref.shape[1]
    pieces = columns // CHUNK

    @pl.loop(0, rows * pieces)
    def _(index):
        row = index // pieces
        start = pl.multiple_of((index % pieces) * CHUNK, 32)
        at = pl.ds(start, CHUNK)
        cells = pl.ds(pl.multiple_of(index * CHUNK, 32), CHUNK)
        grad = stencil(padded, taps_ref, row, start, -1)
        grad = cot_ref[row, at, :].astype(jnp.float32) + grad
        density = density_ref[cells, :]
        density = jnp.concatenate([density] * (grad.shape[1] // density.shape[1]), axis=1)
        cells_ref[cells, :] = (grad / density).astype(jnp.bfloat16)


def back(edges, grad_mixed, taps, cotangent, density):
    rows, columns, width = grad_mixed.shape
    vmem = pl.BlockSpec(memory_space=pltpu.VMEM)
    return pl.pallas_call(
        back_kernel,
        out_shape=jax.ShapeDtypeStruct((rows * columns, width), jnp.bfloat16),
        in_specs=[vmem] * 6,
        out_specs=vmem,
        scratch_shapes=[pltpu.VMEM((rows + 2, columns + 2 * HALO, width), jnp.bfloat16)],
        compiler_params=pltpu.CompilerParams(vmem_limit_bytes=40 << 20),
    )(edges[0], grad_mixed, edges[1], taps, cotangent, density)


def on_device(
    obs_rows,
    obs_instr,
    obs_target,
    obs_cell,
    embed_weight,
    background,
    stencil_taps,
    weight_in,
    weight_out,
    grid_cotangent,
):
    peer_count = lax.axis_size(("tile", "stream"))
    stream = lax.axis_index("stream")
    swap = [(0, 1), (1, 0)]
    rows_dev, features = obs_rows.shape
    instr_dev = embed_weight.shape[0]
    capacity = 2 * rows_dev // peer_count
    lat_rows, lon_cells, width = grid_cotangent.shape
    band_cells = lat_rows * lon_cells
    other_weight = lax.ppermute(embed_weight, "stream", swap)
    weights = jnp.where(
        stream == 0,
        jnp.concatenate([embed_weight, other_weight], axis=0),
        jnp.concatenate([other_weight, embed_weight], axis=0),
    ).reshape(2 * instr_dev * features, width)
    destination = obs_target[:, 0]
    onehot = (destination[:, None] == jnp.arange(peer_count, dtype=jnp.int32)[None, :]).astype(
        jnp.int32
    )
    running = jnp.cumsum(onehot, axis=0)
    totals = running[-1]
    position = jnp.sum((running - onehot) * onehot, axis=1)
    slot_index = destination * capacity + position
    slot_total = peer_count * capacity
    spare = instr_dev * band_cells
    send_rows, send_codes = pack(
        slot_index, obs_instr * band_cells + obs_cell, obs_rows, slot_total
    )
    send_codes = jnp.where(
        jnp.arange(capacity, dtype=jnp.int32)[None, :] < totals[:, None],
        send_codes.reshape(peer_count, capacity),
        spare,
    )
    exchange = functools.partial(
        lax.all_to_all, axis_name=("tile", "stream"), split_axis=0, concat_axis=0, tiled=True
    )
    recv_codes = exchange(send_codes)
    recv_rows = exchange(send_rows.reshape(peer_count, capacity, features))
    held = jnp.sum((recv_codes < spare).astype(jnp.int32), axis=1)
    bounds = (jnp.max(held.reshape(-1, 2), axis=1) + 7) // 8
    recv_cells = jnp.where(recv_codes < spare, recv_codes % band_cells, band_cells)
    sums, field, density = deposit_cells(
        recv_codes.reshape(slot_total),
        recv_cells.reshape(slot_total),
        bounds,
        recv_rows.reshape(slot_total, features),
        weights,
        background,
        instr_dev,
        band_cells,
        capacity,
    )
    field = field.reshape(lat_rows, lon_cells, width)
    grid_output, grad_mixed = layer(
        edge_rows(field), field, stencil_taps, weight_in, weight_out, grid_cotangent
    )
    grad_cells = back(edge_rows(grad_mixed), grad_mixed, stencil_taps, grid_cotangent, density)
    local_grad = lax.dot_general(
        sums,
        grad_cells,
        (((0,), (0,)), ((), ())),
        preferred_element_type=jnp.float32,
    ).reshape(2, instr_dev, features, width)
    keep = jnp.where(stream == 0, local_grad[0], local_grad[1])
    give = jnp.where(stream == 0, local_grad[1], local_grad[0]).astype(jnp.bfloat16)
    group_grad = keep + lax.ppermute(give, "stream", swap).astype(jnp.float32)
    return (grid_output, sum_over_tile(group_grad))


def solution(mesh):
    in_specs = (
        P(("parts", "tile", "stream"), None),
        P(("parts", "tile", "stream")),
        P(("parts", "tile", "stream"), None),
        P(("parts", "tile", "stream")),
        P("stream", None, None),
        P(),
        P(),
        P(),
        P(),
        P(("parts", "tile", "stream"), None, None),
    )
    out_specs = (P(("parts", "tile", "stream"), None, None), P(("parts", "stream"), None, None))
    return jax.shard_map(
        on_device, mesh=mesh, in_specs=in_specs, out_specs=out_specs, check_vma=False
    )
```

```python
import functools

import jax
import jax.numpy as jnp
from jax import lax
from jax.experimental import pallas as pl
from jax.experimental.pallas import tpu as pltpu
from jax.sharding import PartitionSpec as P


def edge_rows(block):
    axes = ("tile", "stream")
    count = lax.axis_size(axes)
    forward = [(i, i + 1) for i in range(count - 1)]
    backward = [(target, source) for source, target in forward]
    return lax.ppermute(block[-1:], axes, forward), lax.ppermute(block[:1], axes, backward)


def pack_kernel(slot_ref, code_ref, rows_ref, out_rows, out_codes, rows_wide, packed):
    rows = rows_ref.shape[0]
    slots = out_rows.shape[0]
    step = 256

    @pl.loop(0, rows // step)
    def _(block):
        at = pl.ds(pl.multiple_of(block * step, step), step)
        rows_wide[at, :] = rows_ref[at, :].astype(jnp.float32)

    @pl.loop(0, slots // step)
    def _(block):
        at = pl.ds(pl.multiple_of(block * step, step), step)
        packed[at, :] = jnp.zeros((step, packed.shape[1]), jnp.float32)

    group = 16

    @pl.loop(0, rows // group)
    def _(block):
        base = block * group
        for inner in range(group):
            slot = slot_ref[base + inner]
            packed[pl.ds(slot, 1), :] = rows_wide[pl.ds(base + inner, 1), :]
            out_codes[slot] = code_ref[base + inner]

    @pl.loop(0, slots // step)
    def _(block):
        at = pl.ds(pl.multiple_of(block * step, step), step)
        out_rows[at, :] = packed[at, :].astype(jnp.bfloat16)


def pack(slot_index, codes, rows, slot_total):
    count, features = rows.shape
    smem = pl.BlockSpec(memory_space=pltpu.SMEM)
    vmem = pl.BlockSpec(memory_space=pltpu.VMEM)
    return pl.pallas_call(
        pack_kernel,
        out_shape=(
            jax.ShapeDtypeStruct((slot_total, features), jnp.bfloat16),
            jax.ShapeDtypeStruct((slot_total,), jnp.int32),
        ),
        in_specs=[smem, smem, vmem],
        out_specs=(vmem, smem),
        scratch_shapes=[
            pltpu.VMEM((count, features), jnp.float32),
            pltpu.VMEM((slot_total, features), jnp.float32),
        ],
        compiler_params=pltpu.CompilerParams(vmem_limit_bytes=24 << 20),
    )(slot_index, codes, rows)


def deposit_kernel(
    instr_dev,
    capacity,
    pitch,
    code_ref,
    cell_ref,
    bound_ref,
    rows_ref,
    weight_ref,
    background_ref,
    sums_out,
    field_out,
    density_out,
    even_sums,
    odd_sums,
    even_count,
    odd_count,
    even_rows,
    odd_rows,
):
    cells = field_out.shape[0]
    features = rows_ref.shape[1]
    pairs = rows_ref.shape[0] // (2 * pitch)
    step = 480

    @pl.loop(0, instr_dev * cells // step)
    def _(block):
        at = pl.ds(pl.multiple_of(block * step, 32), step)
        even_sums[at, :] = jnp.zeros((step, features), jnp.float32)
        odd_sums[at, :] = jnp.zeros((step, features), jnp.float32)

    @pl.loop(0, cells // step)
    def _(block):
        at = pl.ds(pl.multiple_of(block * step, 32), step)
        even_count[at, :] = jnp.zeros((step, features), jnp.float32)
        odd_count[at, :] = jnp.zeros((step, features), jnp.float32)

    one = jnp.ones((1, features), jnp.float32)
    group = 8

    @pl.loop(0, pairs)
    def _(pair):
        first = pl.multiple_of(pair * 2 * capacity, capacity)
        second = pl.multiple_of(first + capacity, capacity)
        even_at = pl.multiple_of(pair * 2 * pitch, 16)
        odd_at = pl.multiple_of(even_at + pitch, 16)
        even_rows[...] = rows_ref[pl.ds(even_at, capacity), :].astype(jnp.float32)
        odd_rows[...] = rows_ref[pl.ds(odd_at, capacity), :].astype(jnp.float32)

        @pl.loop(0, bound_ref[pair])
        def _(block):
            base = block * group
            for inner in range(group):
                place = base + inner
                even_code = code_ref[first + place]
                odd_code = code_ref[second + place]
                even_cell = cell_ref[first + place]
                odd_cell = cell_ref[second + place]
                even_sums[pl.ds(even_code, 1), :] += even_rows[pl.ds(place, 1), :]
                odd_sums[pl.ds(odd_code, 1), :] += odd_rows[pl.ds(place, 1), :]
                even_count[pl.ds(even_cell, 1), :] += one
                odd_count[pl.ds(odd_cell, 1), :] += one

    @pl.loop(0, cells // step)
    def _(block):
        start = pl.multiple_of(block * step, 32)
        at = pl.ds(start, step)
        pieces = []
        for sums in (even_sums, odd_sums):
            for number in range(instr_dev):
                piece = sums[pl.ds(number * cells + start, step), :]
                pieces.append(piece.astype(jnp.bfloat16))
        wide = jnp.concatenate(pieces, axis=1)
        sums_out[at, :] = wide
        deposit = jnp.dot(wide, weight_ref[...], preferred_element_type=jnp.float32)
        density = 1.0 + (even_count[at, :] + odd_count[at, :])
        density_out[at, :] = density
        density = jnp.concatenate([density] * (deposit.shape[1] // features), axis=1)
        field_out[at, :] = ((deposit + background_ref[...]) / density).astype(jnp.bfloat16)


def deposit_cells(
    codes, cells, bounds, rows, weights, background, instr_dev, band_cells, capacity, pitch
):
    features = rows.shape[1]
    width = weights.shape[1]
    smem = pl.BlockSpec(memory_space=pltpu.SMEM)
    vmem = pl.BlockSpec(memory_space=pltpu.VMEM)
    sums = pltpu.VMEM((instr_dev * band_cells + 8, features), jnp.float32)
    counts = pltpu.VMEM((band_cells + 8, features), jnp.float32)
    held = pltpu.VMEM((capacity, features), jnp.float32)
    return pl.pallas_call(
        functools.partial(deposit_kernel, instr_dev, capacity, pitch),
        out_shape=(
            jax.ShapeDtypeStruct((band_cells, weights.shape[0]), jnp.bfloat16),
            jax.ShapeDtypeStruct((band_cells, width), jnp.bfloat16),
            jax.ShapeDtypeStruct((band_cells, features), jnp.float32),
        ),
        in_specs=[smem, smem, smem, vmem, vmem, vmem],
        out_specs=(vmem, vmem, vmem),
        scratch_shapes=[sums, sums, counts, counts, held, held],
        compiler_params=pltpu.CompilerParams(vmem_limit_bytes=58 << 20),
    )(codes, cells, bounds, rows, weights, background.reshape(1, width))


def gathered_over_tile(piece):
    count = lax.axis_size("tile")
    if count & (count - 1):
        return lax.all_gather(piece, "tile")
    me = lax.axis_index("tile")
    distance, axis, block = count // 2, 0, piece
    while distance:
        other = lax.ppermute(block, "tile", [(i, i ^ distance) for i in range(count)])
        upper = (me & distance) > 0
        block = jnp.stack(
            [jnp.where(upper, other, block), jnp.where(upper, block, other)], axis=axis
        )
        axis += 1
        distance //= 2
    return block.reshape((count,) + piece.shape)


HALO = 16
CHUNK = 288


def fill_padded(padded, low_ref, block_ref, high_ref):
    rows, columns = block_ref.shape[0], block_ref.shape[1]
    for row in range(rows + 2):
        if row == 0:
            source, at = low_ref, 0
        elif row == rows + 1:
            source, at = high_ref, 0
        else:
            source, at = block_ref, row - 1
        padded[row, HALO : HALO + columns, :] = source[at]
        padded[row, 0:HALO, :] = source[at, columns - HALO : columns, :]
        padded[row, HALO + columns : 2 * HALO + columns, :] = source[at, 0:HALO, :]


def stencil(padded, taps_ref, row, start, orient):
    size = CHUNK + 2 * HALO
    rows = [
        padded[row + step, pl.ds(start, size), :].astype(jnp.float32) for step in range(3)
    ]
    total = None
    for col_step in range(3):
        summed = None
        for row_step in range(3):
            tap = taps_ref[pl.ds(row_step * 3 + col_step, 1), :]
            term = tap * rows[1 + orient * (row_step - 1)]
            summed = term if summed is None else summed + term
        shift = -orient * (col_step - 1)
        if shift:
            summed = pltpu.roll(summed, shift % size, 0)
        summed = summed[HALO : HALO + CHUNK]
        total = summed if total is None else total + summed
    return total


def layer_kernel(
    low_ref,
    field_ref,
    high_ref,
    taps_ref,
    in_ref,
    out_ref,
    in_t_ref,
    out_t_ref,
    cot_ref,
    grid_ref,
    grad_ref,
    padded,
):
    fill_padded(padded, low_ref, field_ref, high_ref)
    rows, columns = field_ref.shape[0], field_ref.shape[1]
    pieces = columns // CHUNK

    @pl.loop(0, rows * pieces)
    def _(index):
        row = index // pieces
        start = pl.multiple_of((index % pieces) * CHUNK, 32)
        at = pl.ds(start, CHUNK)
        mixed = stencil(padded, taps_ref, row, start, 1)
        inverse = lax.rsqrt(jnp.mean(mixed * mixed, axis=1, keepdims=True) + 1e-06)
        normed = (mixed * inverse).astype(jnp.bfloat16)
        inner = jnp.dot(normed, in_ref[...], preferred_element_type=jnp.float32)
        cot = cot_ref[row, at, :]
        grad_hidden = jnp.dot(cot, out_t_ref[...], preferred_element_type=jnp.float32)
        grad_hidden = grad_hidden.astype(jnp.bfloat16).astype(jnp.float32)
        scale = 0.7978845608028654
        square = inner * inner
        bent = jnp.tanh(inner * (scale + (scale * 0.044715) * square))
        half = 0.5 + 0.5 * bent
        hidden = (inner * half).astype(jnp.bfloat16)
        slope = (2.0 * scale) + (6.0 * scale * 0.044715) * square
        grad_inner = grad_hidden * (half + inner * (half - half * half) * slope)
        result = jnp.dot(hidden, out_ref[...], preferred_element_type=jnp.float32)
        grid_ref[row, at, :] = (field_ref[row, at, :].astype(jnp.float32) + result).astype(
            jnp.bfloat16
        )
        grad_normed = jnp.dot(
            grad_inner.astype(jnp.bfloat16), in_t_ref[...], preferred_element_type=jnp.float32
        )
        grad_normed = grad_normed.astype(jnp.bfloat16).astype(jnp.float32)
        along = jnp.mean(mixed * grad_normed, axis=1, keepdims=True)
        grad_mixed = inverse * grad_normed - mixed * (along * (inverse * inverse * inverse))
        grad_ref[row, at, :] = grad_mixed.astype(jnp.bfloat16)


def layer(edges, field, taps, weight_in, weight_out, cotangent):
    rows, columns, width = field.shape
    vmem = pl.BlockSpec(memory_space=pltpu.VMEM)
    shape = jax.ShapeDtypeStruct(field.shape, jnp.bfloat16)
    return pl.pallas_call(
        layer_kernel,
        out_shape=(shape, shape),
        in_specs=[vmem] * 9,
        out_specs=(vmem, vmem),
        scratch_shapes=[pltpu.VMEM((rows + 2, columns + 2 * HALO, width), jnp.bfloat16)],
        compiler_params=pltpu.CompilerParams(vmem_limit_bytes=40 << 20),
    )(edges[0], field, edges[1], taps, weight_in, weight_out, weight_in.T, weight_out.T, cotangent)


def back_kernel(low_ref, grad_ref, high_ref, taps_ref, cot_ref, density_ref, cells_ref, padded):
    fill_padded(padded, low_ref, grad_ref, high_ref)
    rows, columns = grad_ref.shape[0], grad_ref.shape[1]
    pieces = columns // CHUNK

    @pl.loop(0, rows * pieces)
    def _(index):
        row = index // pieces
        start = pl.multiple_of((index % pieces) * CHUNK, 32)
        at = pl.ds(start, CHUNK)
        cells = pl.ds(pl.multiple_of(index * CHUNK, 32), CHUNK)
        grad = stencil(padded, taps_ref, row, start, -1)
        grad = cot_ref[row, at, :].astype(jnp.float32) + grad
        density = density_ref[cells, :]
        density = jnp.concatenate([density] * (grad.shape[1] // density.shape[1]), axis=1)
        cells_ref[cells, :] = (grad / density).astype(jnp.bfloat16)


def back(edges, grad_mixed, taps, cotangent, density):
    rows, columns, width = grad_mixed.shape
    vmem = pl.BlockSpec(memory_space=pltpu.VMEM)
    return pl.pallas_call(
        back_kernel,
        out_shape=jax.ShapeDtypeStruct((rows * columns, width), jnp.bfloat16),
        in_specs=[vmem] * 6,
        out_specs=vmem,
        scratch_shapes=[pltpu.VMEM((rows + 2, columns + 2 * HALO, width), jnp.bfloat16)],
        compiler_params=pltpu.CompilerParams(vmem_limit_bytes=40 << 20),
    )(edges[0], grad_mixed, edges[1], taps, cotangent, density)


def on_device(
    obs_rows,
    obs_instr,
    obs_target,
    obs_cell,
    embed_weight,
    background,
    stencil_taps,
    weight_in,
    weight_out,
    grid_cotangent,
):
    peer_count = lax.axis_size(("tile", "stream"))
    stream = lax.axis_index("stream")
    swap = [(0, 1), (1, 0)]
    rows_dev, features = obs_rows.shape
    instr_dev = embed_weight.shape[0]
    capacity = 2 * rows_dev // peer_count
    lat_rows, lon_cells, width = grid_cotangent.shape
    band_cells = lat_rows * lon_cells
    other_weight = lax.ppermute(embed_weight, "stream", swap)
    weights = jnp.where(
        stream == 0,
        jnp.concatenate([embed_weight, other_weight], axis=0),
        jnp.concatenate([other_weight, embed_weight], axis=0),
    ).reshape(2 * instr_dev * features, width)
    destination = obs_target[:, 0]
    onehot = (destination[:, None] == jnp.arange(peer_count, dtype=jnp.int32)[None, :]).astype(
        jnp.int32
    )
    running = jnp.cumsum(onehot, axis=0)
    totals = running[-1]
    position = jnp.sum((running - onehot) * onehot, axis=1)
    slot_index = destination * capacity + position
    slot_total = peer_count * capacity
    spare = instr_dev * band_cells
    send_rows, send_codes = pack(
        slot_index, obs_instr * band_cells + obs_cell, obs_rows, slot_total
    )
    send_codes = jnp.where(
        jnp.arange(capacity, dtype=jnp.int32)[None, :] < totals[:, None],
        send_codes.reshape(peer_count, capacity),
        spare,
    )
    code_rows = capacity // features
    padding = -2 * code_rows % 16
    coded = jnp.concatenate(
        [
            (send_codes // 256).reshape(peer_count, code_rows, features),
            (send_codes % 256).reshape(peer_count, code_rows, features),
            jnp.zeros((peer_count, padding, features), jnp.int32),
        ],
        axis=1,
    ).astype(jnp.bfloat16)
    recv_rows = lax.all_to_all(
        jnp.concatenate([send_rows.reshape(peer_count, capacity, features), coded], axis=1),
        ("tile", "stream"),
        split_axis=0,
        concat_axis=0,
        tiled=True,
    )
    pitch = capacity + 2 * code_rows + padding
    digits = recv_rows[:, capacity : capacity + 2 * code_rows].astype(jnp.int32)
    recv_codes = (digits[:, :code_rows] * 256 + digits[:, code_rows:]).reshape(
        peer_count, capacity
    )
    held = jnp.sum((recv_codes < spare).astype(jnp.int32), axis=1)
    bounds = (jnp.max(held.reshape(-1, 2), axis=1) + 7) // 8
    recv_cells = jnp.where(recv_codes < spare, recv_codes % band_cells, band_cells)
    sums, field, density = deposit_cells(
        recv_codes.reshape(slot_total),
        recv_cells.reshape(slot_total),
        bounds,
        recv_rows.reshape(peer_count * pitch, features),
        weights,
        background,
        instr_dev,
        band_cells,
        capacity,
        pitch,
    )
    field = field.reshape(lat_rows, lon_cells, width)
    grid_output, grad_mixed = layer(
        edge_rows(field), field, stencil_taps, weight_in, weight_out, grid_cotangent
    )
    grad_cells = back(edge_rows(grad_mixed), grad_mixed, stencil_taps, grid_cotangent, density)
    local_grad = lax.dot_general(
        sums,
        grad_cells,
        (((0,), (0,)), ((), ())),
        preferred_element_type=jnp.float32,
    )
    tiles = peer_count // 2
    shares = local_grad.astype(jnp.bfloat16).reshape(2, tiles, -1, width)
    shares = lax.all_to_all(
        jnp.swapaxes(shares, 0, 1).reshape(peer_count, -1, width),
        ("tile", "stream"),
        split_axis=0,
        concat_axis=0,
        tiled=True,
    )
    piece = jnp.sum(shares.astype(jnp.float32), axis=0).astype(jnp.bfloat16)
    embed_grad = gathered_over_tile(piece).astype(jnp.float32)
    return (grid_output, embed_grad.reshape(embed_weight.shape))


def solution(mesh):
    in_specs = (
        P(("parts", "tile", "stream"), None),
        P(("parts", "tile", "stream")),
        P(("parts", "tile", "stream"), None),
        P(("parts", "tile", "stream")),
        P("stream", None, None),
        P(),
        P(),
        P(),
        P(),
        P(("parts", "tile", "stream"), None, None),
    )
    out_specs = (P(("parts", "tile", "stream"), None, None), P(("parts", "stream"), None, None))
    return jax.shard_map(
        on_device, mesh=mesh, in_specs=in_specs, out_specs=out_specs, check_vma=False
    )
```

```python
import functools

import jax
import jax.numpy as jnp
from jax import lax
from jax.experimental import pallas as pl
from jax.experimental.pallas import tpu as pltpu
from jax.sharding import PartitionSpec as P


def edge_rows(first, last):
    axes = ("tile", "stream")
    count = lax.axis_size(axes)
    forward = [(i, i + 1) for i in range(count - 1)]
    backward = [(target, source) for source, target in forward]
    return lax.ppermute(last, axes, forward), lax.ppermute(first, axes, backward)


def pack_kernel(slot_ref, code_ref, rows_ref, out_rows, out_codes, rows_wide, packed):
    rows = rows_ref.shape[0]
    slots = out_rows.shape[0]
    step = 256

    @pl.loop(0, rows // step)
    def _(block):
        at = pl.ds(pl.multiple_of(block * step, step), step)
        rows_wide[at, :] = rows_ref[at, :].astype(jnp.float32)

    @pl.loop(0, slots // step)
    def _(block):
        at = pl.ds(pl.multiple_of(block * step, step), step)
        packed[at, :] = jnp.zeros((step, packed.shape[1]), jnp.float32)

    group = 16

    @pl.loop(0, rows // group)
    def _(block):
        base = block * group
        for inner in range(group):
            slot = slot_ref[base + inner]
            packed[pl.ds(slot, 1), :] = rows_wide[pl.ds(base + inner, 1), :]
            out_codes[slot] = code_ref[base + inner]

    @pl.loop(0, slots // step)
    def _(block):
        at = pl.ds(pl.multiple_of(block * step, step), step)
        out_rows[at, :] = packed[at, :].astype(jnp.bfloat16)


def pack(slot_index, codes, rows, slot_total):
    count, features = rows.shape
    smem = pl.BlockSpec(memory_space=pltpu.SMEM)
    vmem = pl.BlockSpec(memory_space=pltpu.VMEM)
    return pl.pallas_call(
        pack_kernel,
        out_shape=(
            jax.ShapeDtypeStruct((slot_total, features), jnp.bfloat16),
            jax.ShapeDtypeStruct((slot_total,), jnp.int32),
        ),
        in_specs=[smem, smem, vmem],
        out_specs=(vmem, smem),
        scratch_shapes=[
            pltpu.VMEM((count, features), jnp.float32),
            pltpu.VMEM((slot_total, features), jnp.float32),
        ],
        compiler_params=pltpu.CompilerParams(vmem_limit_bytes=24 << 20),
    )(slot_index, codes, rows)


def deposit_kernel(
    instr_dev,
    capacity,
    pitch,
    code_ref,
    cell_ref,
    bound_ref,
    rows_ref,
    weight_ref,
    background_ref,
    sums_out,
    field_out,
    density_out,
    even_sums,
    odd_sums,
    even_count,
    odd_count,
    even_rows,
    odd_rows,
):
    cells = field_out.shape[0]
    features = rows_ref.shape[1]
    pairs = rows_ref.shape[0] // (2 * pitch)
    step = 480

    @pl.loop(0, instr_dev * cells // step)
    def _(block):
        at = pl.ds(pl.multiple_of(block * step, 32), step)
        even_sums[at, :] = jnp.zeros((step, features), jnp.float32)
        odd_sums[at, :] = jnp.zeros((step, features), jnp.float32)

    @pl.loop(0, cells // step)
    def _(block):
        at = pl.ds(pl.multiple_of(block * step, 32), step)
        even_count[at, :] = jnp.zeros((step, features), jnp.float32)
        odd_count[at, :] = jnp.zeros((step, features), jnp.float32)

    one = jnp.ones((1, features), jnp.float32)
    group = 8

    @pl.loop(0, pairs)
    def _(pair):
        first = pl.multiple_of(pair * 2 * capacity, capacity)
        second = pl.multiple_of(first + capacity, capacity)
        even_at = pl.multiple_of(pair * 2 * pitch, 16)
        odd_at = pl.multiple_of(even_at + pitch, 16)
        even_rows[...] = rows_ref[pl.ds(even_at, capacity), :].astype(jnp.float32)
        odd_rows[...] = rows_ref[pl.ds(odd_at, capacity), :].astype(jnp.float32)

        @pl.loop(0, bound_ref[pair])
        def _(block):
            base = block * group
            for inner in range(group):
                place = base + inner
                even_code = code_ref[first + place]
                odd_code = code_ref[second + place]
                even_cell = cell_ref[first + place]
                odd_cell = cell_ref[second + place]
                even_sums[pl.ds(even_code, 1), :] += even_rows[pl.ds(place, 1), :]
                odd_sums[pl.ds(odd_code, 1), :] += odd_rows[pl.ds(place, 1), :]
                even_count[pl.ds(even_cell, 1), :] += one
                odd_count[pl.ds(odd_cell, 1), :] += one

    @pl.loop(0, cells // step)
    def _(block):
        start = pl.multiple_of(block * step, 32)
        at = pl.ds(start, step)
        pieces = []
        for sums in (even_sums, odd_sums):
            for number in range(instr_dev):
                piece = sums[pl.ds(number * cells + start, step), :]
                pieces.append(piece.astype(jnp.bfloat16))
        wide = jnp.concatenate(pieces, axis=1)
        sums_out[at, :] = wide
        deposit = jnp.dot(wide, weight_ref[...], preferred_element_type=jnp.float32)
        density = 1.0 + (even_count[at, :] + odd_count[at, :])
        density_out[at, :] = density
        density = jnp.concatenate([density] * (deposit.shape[1] // features), axis=1)
        field_out[at, :] = ((deposit + background_ref[...]) / density).astype(jnp.bfloat16)


def deposit_cells(
    codes, cells, bounds, rows, weights, background, instr_dev, band_cells, capacity, pitch
):
    features = rows.shape[1]
    width = weights.shape[1]
    smem = pl.BlockSpec(memory_space=pltpu.SMEM)
    vmem = pl.BlockSpec(memory_space=pltpu.VMEM)
    sums = pltpu.VMEM((instr_dev * band_cells + 8, features), jnp.float32)
    counts = pltpu.VMEM((band_cells + 8, features), jnp.float32)
    held = pltpu.VMEM((capacity, features), jnp.float32)
    return pl.pallas_call(
        functools.partial(deposit_kernel, instr_dev, capacity, pitch),
        out_shape=(
            jax.ShapeDtypeStruct((band_cells, weights.shape[0]), jnp.bfloat16),
            jax.ShapeDtypeStruct((band_cells, width), jnp.bfloat16),
            jax.ShapeDtypeStruct((band_cells, features), jnp.float32),
        ),
        in_specs=[smem, smem, smem, vmem, vmem, vmem],
        out_specs=(vmem, vmem, vmem),
        scratch_shapes=[sums, sums, counts, counts, held, held],
        compiler_params=pltpu.CompilerParams(vmem_limit_bytes=58 << 20),
    )(codes, cells, bounds, rows, weights, background.reshape(1, width))


def gathered_over_tile(piece):
    count = lax.axis_size("tile")
    if count & (count - 1):
        return lax.all_gather(piece, "tile")
    me = lax.axis_index("tile")
    distance, axis, block = count // 2, 0, piece
    while distance:
        other = lax.ppermute(block, "tile", [(i, i ^ distance) for i in range(count)])
        upper = (me & distance) > 0
        block = jnp.stack(
            [jnp.where(upper, other, block), jnp.where(upper, block, other)], axis=axis
        )
        axis += 1
        distance //= 2
    return block.reshape((count,) + piece.shape)


HALO = 16
CHUNK = 288


def fill_padded(padded, sources):
    for row, (source, at) in enumerate(sources):
        columns = source.shape[1]
        padded[row, HALO : HALO + columns, :] = source[at]
        padded[row, 0:HALO, :] = source[at, columns - HALO : columns, :]
        padded[row, HALO + columns : 2 * HALO + columns, :] = source[at, 0:HALO, :]


def stencil(padded, taps_ref, row, start, orient):
    size = CHUNK + 2 * HALO
    rows = [
        padded[row + step, pl.ds(start, size), :].astype(jnp.float32) for step in range(3)
    ]
    total = None
    for col_step in range(3):
        summed = None
        for row_step in range(3):
            tap = taps_ref[pl.ds(row_step * 3 + col_step, 1), :]
            term = tap * rows[1 + orient * (row_step - 1)]
            summed = term if summed is None else summed + term
        shift = -orient * (col_step - 1)
        if shift:
            summed = pltpu.roll(summed, shift % size, 0)
        summed = summed[HALO : HALO + CHUNK]
        total = summed if total is None else total + summed
    return total


def layer_kernel(edge, *refs):
    if edge:
        low_ref, high_ref, *refs = refs
    field_ref, taps_ref, in_ref, out_ref, in_t_ref, out_t_ref, cot_ref, *refs = refs
    grid_ref, grad_ref, padded = refs
    lat_rows, columns = field_ref.shape[0], field_ref.shape[1]
    inside = [(field_ref, row) for row in range(lat_rows)]
    if edge:
        fill_padded(padded, [(low_ref, 0)] + inside[:2] + inside[-2:] + [(high_ref, 0)])
    else:
        fill_padded(padded, inside)
    rows = grid_ref.shape[0]
    pieces = columns // CHUNK

    @pl.loop(0, rows * pieces)
    def _(index):
        row = index // pieces
        band_row = row * (lat_rows - 1) if edge else row + 1
        start = pl.multiple_of((index % pieces) * CHUNK, 32)
        at = pl.ds(start, CHUNK)
        mixed = stencil(padded, taps_ref, 3 * row if edge else row, start, 1)
        inverse = lax.rsqrt(jnp.mean(mixed * mixed, axis=1, keepdims=True) + 1e-06)
        normed = (mixed * inverse).astype(jnp.bfloat16)
        inner = jnp.dot(normed, in_ref[...], preferred_element_type=jnp.float32)
        cot = cot_ref[band_row, at, :]
        grad_hidden = jnp.dot(cot, out_t_ref[...], preferred_element_type=jnp.float32)
        grad_hidden = grad_hidden.astype(jnp.bfloat16).astype(jnp.float32)
        scale = 0.7978845608028654
        square = inner * inner
        bent = jnp.tanh(inner * (scale + (scale * 0.044715) * square))
        half = 0.5 + 0.5 * bent
        hidden = (inner * half).astype(jnp.bfloat16)
        slope = (2.0 * scale) + (6.0 * scale * 0.044715) * square
        grad_inner = grad_hidden * (half + inner * (half - half * half) * slope)
        result = jnp.dot(hidden, out_ref[...], preferred_element_type=jnp.float32)
        grid_ref[row, at, :] = (field_ref[band_row, at, :].astype(jnp.float32) + result).astype(
            jnp.bfloat16
        )
        grad_normed = jnp.dot(
            grad_inner.astype(jnp.bfloat16), in_t_ref[...], preferred_element_type=jnp.float32
        )
        grad_normed = grad_normed.astype(jnp.bfloat16).astype(jnp.float32)
        along = jnp.mean(mixed * grad_normed, axis=1, keepdims=True)
        grad_mixed = inverse * grad_normed - mixed * (along * (inverse * inverse * inverse))
        grad_ref[row, at, :] = grad_mixed.astype(jnp.bfloat16)


def layer(edges, field, taps, weights, cotangent):
    lat_rows, columns, width = field.shape
    edge = len(edges) > 0
    rows = 2 if edge else lat_rows - 2
    vmem = pl.BlockSpec(memory_space=pltpu.VMEM)
    shape = jax.ShapeDtypeStruct((rows, columns, width), jnp.bfloat16)
    depth = 6 if edge else lat_rows
    return pl.pallas_call(
        functools.partial(layer_kernel, edge),
        out_shape=(shape, shape),
        in_specs=[vmem] * (len(edges) + 7),
        out_specs=(vmem, vmem),
        scratch_shapes=[pltpu.VMEM((depth, columns + 2 * HALO, width), jnp.bfloat16)],
        cost_estimate=pl.CostEstimate(
            flops=8 * rows * columns * weights[0].size,
            bytes_accessed=8 * rows * columns * width,
            transcendentals=rows * columns * weights[0].shape[1],
        ),
        compiler_params=pltpu.CompilerParams(vmem_limit_bytes=36 << 20),
    )(*edges, field, taps, *weights, cotangent)


def back_kernel(edge, *refs):
    if edge:
        low_ref, high_ref, *refs = refs
    edge_ref, mid_ref, taps_ref, cot_ref, density_ref, cells_ref, padded = refs
    lat_rows, columns = cot_ref.shape[0], cot_ref.shape[1]
    inside = [(edge_ref, 0)] + [(mid_ref, row) for row in range(lat_rows - 2)] + [(edge_ref, 1)]
    if edge:
        fill_padded(padded, [(low_ref, 0)] + inside[:2] + inside[-2:] + [(high_ref, 0)])
    else:
        fill_padded(padded, inside)
    rows = cells_ref.shape[0] // columns
    pieces = columns // CHUNK

    @pl.loop(0, rows * pieces)
    def _(index):
        row = index // pieces
        band_row = row * (lat_rows - 1) if edge else row + 1
        start = pl.multiple_of((index % pieces) * CHUNK, 32)
        at = pl.ds(start, CHUNK)
        cells = pl.ds(pl.multiple_of(index * CHUNK, 32), CHUNK)
        held = pl.ds(pl.multiple_of(band_row * columns + start, 32), CHUNK)
        grad = stencil(padded, taps_ref, 3 * row if edge else row, start, -1)
        grad = cot_ref[band_row, at, :].astype(jnp.float32) + grad
        density = density_ref[held, :]
        density = jnp.concatenate([density] * (grad.shape[1] // density.shape[1]), axis=1)
        cells_ref[cells, :] = (grad / density).astype(jnp.bfloat16)


def back(edges, grad_edge, grad_mid, taps, cotangent, density):
    lat_rows, columns, width = cotangent.shape
    edge = len(edges) > 0
    rows = 2 if edge else lat_rows - 2
    vmem = pl.BlockSpec(memory_space=pltpu.VMEM)
    depth = 6 if edge else lat_rows
    return pl.pallas_call(
        functools.partial(back_kernel, edge),
        out_shape=jax.ShapeDtypeStruct((rows * columns, width), jnp.bfloat16),
        in_specs=[vmem] * (len(edges) + 5),
        out_specs=vmem,
        scratch_shapes=[pltpu.VMEM((depth, columns + 2 * HALO, width), jnp.bfloat16)],
        cost_estimate=pl.CostEstimate(
            flops=40 * rows * columns * width,
            bytes_accessed=10 * rows * columns * width,
            transcendentals=0,
        ),
        compiler_params=pltpu.CompilerParams(vmem_limit_bytes=36 << 20),
    )(*edges, grad_edge, grad_mid, taps, cotangent, density)


def outer_sum(sums, cells):
    return lax.dot_general(
        sums, cells, (((0,), (0,)), ((), ())), preferred_element_type=jnp.float32
    )


def on_device(
    obs_rows,
    obs_instr,
    obs_target,
    obs_cell,
    embed_weight,
    background,
    stencil_taps,
    weight_in,
    weight_out,
    grid_cotangent,
):
    peer_count = lax.axis_size(("tile", "stream"))
    stream = lax.axis_index("stream")
    swap = [(0, 1), (1, 0)]
    rows_dev, features = obs_rows.shape
    instr_dev = embed_weight.shape[0]
    capacity = 2 * rows_dev // peer_count
    lat_rows, lon_cells, width = grid_cotangent.shape
    band_cells = lat_rows * lon_cells
    other_weight = lax.ppermute(embed_weight, "stream", swap)
    weights = jnp.where(
        stream == 0,
        jnp.concatenate([embed_weight, other_weight], axis=0),
        jnp.concatenate([other_weight, embed_weight], axis=0),
    ).reshape(2 * instr_dev * features, width)
    destination = obs_target[:, 0]
    onehot = (destination[:, None] == jnp.arange(peer_count, dtype=jnp.int32)[None, :]).astype(
        jnp.int32
    )
    running = jnp.cumsum(onehot, axis=0)
    totals = running[-1]
    position = jnp.sum((running - onehot) * onehot, axis=1)
    slot_index = destination * capacity + position
    slot_total = peer_count * capacity
    spare = instr_dev * band_cells
    send_rows, send_codes = pack(
        slot_index, obs_instr * band_cells + obs_cell, obs_rows, slot_total
    )
    send_codes = jnp.where(
        jnp.arange(capacity, dtype=jnp.int32)[None, :] < totals[:, None],
        send_codes.reshape(peer_count, capacity),
        spare,
    )
    code_rows = capacity // features
    padding = -2 * code_rows % 16
    coded = jnp.concatenate(
        [
            (send_codes // 256).reshape(peer_count, code_rows, features),
            (send_codes % 256).reshape(peer_count, code_rows, features),
            jnp.zeros((peer_count, padding, features), jnp.int32),
        ],
        axis=1,
    ).astype(jnp.bfloat16)
    recv_rows = lax.all_to_all(
        jnp.concatenate([send_rows.reshape(peer_count, capacity, features), coded], axis=1),
        ("tile", "stream"),
        split_axis=0,
        concat_axis=0,
        tiled=True,
    )
    pitch = capacity + 2 * code_rows + padding
    digits = recv_rows[:, capacity : capacity + 2 * code_rows].astype(jnp.int32)
    recv_codes = (digits[:, :code_rows] * 256 + digits[:, code_rows:]).reshape(
        peer_count, capacity
    )
    held = jnp.sum((recv_codes < spare).astype(jnp.int32), axis=1)
    bounds = (jnp.max(held.reshape(-1, 2), axis=1) + 7) // 8
    recv_cells = jnp.where(recv_codes < spare, recv_codes % band_cells, band_cells)
    sums, field, density = deposit_cells(
        recv_codes.reshape(slot_total),
        recv_cells.reshape(slot_total),
        bounds,
        recv_rows.reshape(peer_count * pitch, features),
        weights,
        background,
        instr_dev,
        band_cells,
        capacity,
        pitch,
    )
    field = field.reshape(lat_rows, lon_cells, width)
    matrices = (weight_in, weight_out, weight_in.T, weight_out.T)
    edges = edge_rows(field[:1], field[-1:])
    mid_output, mid_grad = layer((), field, stencil_taps, matrices, grid_cotangent)
    edge_output, edge_grad = layer(edges, field, stencil_taps, matrices, grid_cotangent)
    grad_edges = edge_rows(edge_grad[:1], edge_grad[1:])
    grid_output = jnp.concatenate([edge_output[:1], mid_output, edge_output[1:]], axis=0)
    mid_cells = back((), edge_grad, mid_grad, stencil_taps, grid_cotangent, density)
    local_grad = outer_sum(sums[lon_cells : band_cells - lon_cells], mid_cells)
    edge_cells = back(grad_edges, edge_grad, mid_grad, stencil_taps, grid_cotangent, density)
    local_grad = local_grad + outer_sum(sums[:lon_cells], edge_cells[:lon_cells])
    local_grad = local_grad + outer_sum(sums[band_cells - lon_cells :], edge_cells[lon_cells:])
    tiles = peer_count // 2
    shares = local_grad.astype(jnp.bfloat16).reshape(2, tiles, -1, width)
    shares = lax.all_to_all(
        jnp.swapaxes(shares, 0, 1).reshape(peer_count, -1, width),
        ("tile", "stream"),
        split_axis=0,
        concat_axis=0,
        tiled=True,
    )
    piece = jnp.sum(shares.astype(jnp.float32), axis=0).astype(jnp.bfloat16)
    embed_grad = gathered_over_tile(piece).astype(jnp.float32)
    return (grid_output, embed_grad.reshape(embed_weight.shape))


def solution(mesh):
    in_specs = (
        P(("parts", "tile", "stream"), None),
        P(("parts", "tile", "stream")),
        P(("parts", "tile", "stream"), None),
        P(("parts", "tile", "stream")),
        P("stream", None, None),
        P(),
        P(),
        P(),
        P(),
        P(("parts", "tile", "stream"), None, None),
    )
    out_specs = (P(("parts", "tile", "stream"), None, None), P(("parts", "stream"), None, None))
    return jax.shard_map(
        on_device, mesh=mesh, in_specs=in_specs, out_specs=out_specs, check_vma=False
    )
```

```python
import functools

import jax
import jax.numpy as jnp
from jax import lax
from jax.experimental import pallas as pl
from jax.experimental.pallas import tpu as pltpu
from jax.sharding import PartitionSpec as P


def edge_rows(first, last):
    axes = ("tile", "stream")
    count = lax.axis_size(axes)
    forward = [(i, i + 1) for i in range(count - 1)]
    backward = [(target, source) for source, target in forward]
    return lax.ppermute(last, axes, forward), lax.ppermute(first, axes, backward)


def pack_kernel(slot_ref, code_ref, rows_ref, out_rows, out_codes, rows_wide, packed):
    rows = rows_ref.shape[0]
    slots = out_rows.shape[0]
    step = 256

    @pl.loop(0, rows // step)
    def _(block):
        at = pl.ds(pl.multiple_of(block * step, step), step)
        rows_wide[at, :] = rows_ref[at, :].astype(jnp.float32)

    @pl.loop(0, slots // step)
    def _(block):
        at = pl.ds(pl.multiple_of(block * step, step), step)
        packed[at, :] = jnp.zeros((step, packed.shape[1]), jnp.float32)

    group = 16

    @pl.loop(0, rows // group)
    def _(block):
        base = block * group
        for inner in range(group):
            slot = slot_ref[base + inner]
            packed[pl.ds(slot, 1), :] = rows_wide[pl.ds(base + inner, 1), :]
            out_codes[slot] = code_ref[base + inner]

    @pl.loop(0, slots // step)
    def _(block):
        at = pl.ds(pl.multiple_of(block * step, step), step)
        out_rows[at, :] = packed[at, :].astype(jnp.bfloat16)


def pack(slot_index, codes, rows, slot_total):
    count, features = rows.shape
    smem = pl.BlockSpec(memory_space=pltpu.SMEM)
    vmem = pl.BlockSpec(memory_space=pltpu.VMEM)
    return pl.pallas_call(
        pack_kernel,
        out_shape=(
            jax.ShapeDtypeStruct((slot_total, features), jnp.bfloat16),
            jax.ShapeDtypeStruct((slot_total,), jnp.int32),
        ),
        in_specs=[smem, smem, vmem],
        out_specs=(vmem, smem),
        scratch_shapes=[
            pltpu.VMEM((count, features), jnp.float32),
            pltpu.VMEM((slot_total, features), jnp.float32),
        ],
        compiler_params=pltpu.CompilerParams(vmem_limit_bytes=24 << 20),
    )(slot_index, codes, rows)


def deposit_kernel(
    instr_dev,
    capacity,
    pitch,
    code_ref,
    cell_ref,
    bound_ref,
    rows_ref,
    weight_ref,
    background_ref,
    sums_out,
    field_out,
    density_out,
    even_sums,
    odd_sums,
    even_count,
    odd_count,
    even_rows,
    odd_rows,
):
    cells = field_out.shape[0]
    features = rows_ref.shape[1]
    pairs = rows_ref.shape[0] // (2 * pitch)
    step = 480

    @pl.loop(0, instr_dev * cells // step)
    def _(block):
        at = pl.ds(pl.multiple_of(block * step, 32), step)
        even_sums[at, :] = jnp.zeros((step, features), jnp.float32)
        odd_sums[at, :] = jnp.zeros((step, features), jnp.float32)

    @pl.loop(0, cells // step)
    def _(block):
        at = pl.ds(pl.multiple_of(block * step, 32), step)
        even_count[at, :] = jnp.zeros((step, features), jnp.float32)
        odd_count[at, :] = jnp.zeros((step, features), jnp.float32)

    one = jnp.ones((1, features), jnp.float32)
    group = 8

    @pl.loop(0, pairs)
    def _(pair):
        first = pl.multiple_of(pair * 2 * capacity, capacity)
        second = pl.multiple_of(first + capacity, capacity)
        even_at = pl.multiple_of(pair * 2 * pitch, 16)
        odd_at = pl.multiple_of(even_at + pitch, 16)
        even_rows[...] = rows_ref[pl.ds(even_at, capacity), :].astype(jnp.float32)
        odd_rows[...] = rows_ref[pl.ds(odd_at, capacity), :].astype(jnp.float32)

        @pl.loop(0, bound_ref[pair])
        def _(block):
            base = block * group
            for inner in range(group):
                place = base + inner
                even_code = code_ref[first + place]
                odd_code = code_ref[second + place]
                even_cell = cell_ref[first + place]
                odd_cell = cell_ref[second + place]
                even_sums[pl.ds(even_code, 1), :] += even_rows[pl.ds(place, 1), :]
                odd_sums[pl.ds(odd_code, 1), :] += odd_rows[pl.ds(place, 1), :]
                even_count[pl.ds(even_cell, 1), :] += one
                odd_count[pl.ds(odd_cell, 1), :] += one

    @pl.loop(0, cells // step)
    def _(block):
        start = pl.multiple_of(block * step, 32)
        at = pl.ds(start, step)
        pieces = []
        for sums in (even_sums, odd_sums):
            for number in range(instr_dev):
                piece = sums[pl.ds(number * cells + start, step), :]
                pieces.append(piece.astype(jnp.bfloat16))
        wide = jnp.concatenate(pieces, axis=1)
        sums_out[at, :] = wide
        deposit = jnp.dot(wide, weight_ref[...], preferred_element_type=jnp.float32)
        density = 1.0 + (even_count[at, :] + odd_count[at, :])
        density_out[at, :] = density
        density = jnp.concatenate([density] * (deposit.shape[1] // features), axis=1)
        field_out[at, :] = ((deposit + background_ref[...]) / density).astype(jnp.bfloat16)


def deposit_cells(
    codes, cells, bounds, rows, weights, background, instr_dev, band_cells, capacity, pitch
):
    features = rows.shape[1]
    width = weights.shape[1]
    smem = pl.BlockSpec(memory_space=pltpu.SMEM)
    vmem = pl.BlockSpec(memory_space=pltpu.VMEM)
    sums = pltpu.VMEM((instr_dev * band_cells + 8, features), jnp.float32)
    counts = pltpu.VMEM((band_cells + 8, features), jnp.float32)
    held = pltpu.VMEM((capacity, features), jnp.float32)
    return pl.pallas_call(
        functools.partial(deposit_kernel, instr_dev, capacity, pitch),
        out_shape=(
            jax.ShapeDtypeStruct((band_cells, weights.shape[0]), jnp.bfloat16),
            jax.ShapeDtypeStruct((band_cells, width), jnp.bfloat16),
            jax.ShapeDtypeStruct((band_cells, features), jnp.float32),
        ),
        in_specs=[smem, smem, smem, vmem, vmem, vmem],
        out_specs=(vmem, vmem, vmem),
        scratch_shapes=[sums, sums, counts, counts, held, held],
        compiler_params=pltpu.CompilerParams(vmem_limit_bytes=58 << 20),
    )(codes, cells, bounds, rows, weights, background.reshape(1, width))


def gathered_over_tile(piece):
    count = lax.axis_size("tile")
    if count & (count - 1):
        return lax.all_gather(piece, "tile")
    me = lax.axis_index("tile")
    distance, axis, block = count // 2, 0, piece
    while distance:
        other = lax.ppermute(block, "tile", [(i, i ^ distance) for i in range(count)])
        upper = (me & distance) > 0
        block = jnp.stack(
            [jnp.where(upper, other, block), jnp.where(upper, block, other)], axis=axis
        )
        axis += 1
        distance //= 2
    return block.reshape((count,) + piece.shape)


HALO = 16
CHUNK = 288


def fill_padded(padded, sources):
    for row, (source, at) in enumerate(sources):
        columns = source.shape[1]
        padded[row, HALO : HALO + columns, :] = source[at]
        padded[row, 0:HALO, :] = source[at, columns - HALO : columns, :]
        padded[row, HALO + columns : 2 * HALO + columns, :] = source[at, 0:HALO, :]


def stencil(padded, taps_ref, row, start, orient):
    size = CHUNK + 2 * HALO
    rows = [
        padded[row + step, pl.ds(start, size), :].astype(jnp.float32) for step in range(3)
    ]
    total = None
    for col_step in range(3):
        summed = None
        for row_step in range(3):
            tap = taps_ref[pl.ds(row_step * 3 + col_step, 1), :]
            term = tap * rows[1 + orient * (row_step - 1)]
            summed = term if summed is None else summed + term
        shift = -orient * (col_step - 1)
        if shift:
            summed = pltpu.roll(summed, shift % size, 0)
        summed = summed[HALO : HALO + CHUNK]
        total = summed if total is None else total + summed
    return total


def layer_kernel(edge, *refs):
    if edge:
        low_ref, high_ref, *refs = refs
    field_ref, taps_ref, in_ref, out_ref, in_t_ref, out_t_ref, cot_ref, *refs = refs
    grid_ref, grad_ref, padded = refs
    lat_rows, columns = field_ref.shape[0], field_ref.shape[1]
    inside = [(field_ref, row) for row in range(lat_rows)]
    if edge:
        fill_padded(padded, [(low_ref, 0)] + inside[:2] + inside[-2:] + [(high_ref, 0)])
    else:
        fill_padded(padded, inside)
    rows = grid_ref.shape[0]
    pieces = columns // CHUNK

    @pl.loop(0, rows * pieces)
    def _(index):
        row = index // pieces
        band_row = row * (lat_rows - 1) if edge else row + 1
        start = pl.multiple_of((index % pieces) * CHUNK, 32)
        at = pl.ds(start, CHUNK)
        mixed = stencil(padded, taps_ref, 3 * row if edge else row, start, 1)
        inverse = lax.rsqrt(jnp.mean(mixed * mixed, axis=1, keepdims=True) + 1e-06)
        normed = (mixed * inverse).astype(jnp.bfloat16)
        inner = jnp.dot(normed, in_ref[...], preferred_element_type=jnp.float32)
        cot = cot_ref[band_row, at, :]
        grad_hidden = jnp.dot(cot, out_t_ref[...], preferred_element_type=jnp.float32)
        grad_hidden = grad_hidden.astype(jnp.bfloat16).astype(jnp.float32)
        scale = 0.7978845608028654
        square = inner * inner
        bent = jnp.tanh(inner * (scale + (scale * 0.044715) * square))
        half = 0.5 + 0.5 * bent
        hidden = (inner * half).astype(jnp.bfloat16)
        slope = (2.0 * scale) + (6.0 * scale * 0.044715) * square
        grad_inner = grad_hidden * (half + inner * (half - half * half) * slope)
        result = jnp.dot(hidden, out_ref[...], preferred_element_type=jnp.float32)
        grid_ref[row, at, :] = (field_ref[band_row, at, :].astype(jnp.float32) + result).astype(
            jnp.bfloat16
        )
        grad_normed = jnp.dot(
            grad_inner.astype(jnp.bfloat16), in_t_ref[...], preferred_element_type=jnp.float32
        )
        grad_normed = grad_normed.astype(jnp.bfloat16).astype(jnp.float32)
        along = jnp.mean(mixed * grad_normed, axis=1, keepdims=True)
        grad_mixed = inverse * grad_normed - mixed * (along * (inverse * inverse * inverse))
        grad_ref[row, at, :] = grad_mixed.astype(jnp.bfloat16)


def layer(edges, field, taps, weights, cotangent):
    lat_rows, columns, width = field.shape
    edge = len(edges) > 0
    rows = 2 if edge else lat_rows - 2
    vmem = pl.BlockSpec(memory_space=pltpu.VMEM)
    shape = jax.ShapeDtypeStruct((rows, columns, width), jnp.bfloat16)
    depth = 6 if edge else lat_rows
    return pl.pallas_call(
        functools.partial(layer_kernel, edge),
        out_shape=(shape, shape),
        in_specs=[vmem] * (len(edges) + 7),
        out_specs=(vmem, vmem),
        scratch_shapes=[pltpu.VMEM((depth, columns + 2 * HALO, width), jnp.bfloat16)],
        cost_estimate=pl.CostEstimate(
            flops=8 * rows * columns * weights[0].size,
            bytes_accessed=8 * rows * columns * width,
            transcendentals=rows * columns * weights[0].shape[1],
        ),
        compiler_params=pltpu.CompilerParams(vmem_limit_bytes=36 << 20),
    )(*edges, field, taps, *weights, cotangent)


def back_kernel(edge, *refs):
    if edge:
        low_ref, high_ref, *refs = refs
    edge_ref, mid_ref, taps_ref, cot_ref, density_ref, cells_ref, padded = refs
    lat_rows, columns = cot_ref.shape[0], cot_ref.shape[1]
    inside = [(edge_ref, 0)] + [(mid_ref, row) for row in range(lat_rows - 2)] + [(edge_ref, 1)]
    if edge:
        fill_padded(padded, [(low_ref, 0)] + inside[:2] + inside[-2:] + [(high_ref, 0)])
    else:
        fill_padded(padded, inside)
    rows = cells_ref.shape[0] // columns
    pieces = columns // CHUNK

    @pl.loop(0, rows * pieces)
    def _(index):
        row = index // pieces
        band_row = row * (lat_rows - 1) if edge else row + 1
        start = pl.multiple_of((index % pieces) * CHUNK, 32)
        at = pl.ds(start, CHUNK)
        cells = pl.ds(pl.multiple_of(index * CHUNK, 32), CHUNK)
        held = pl.ds(pl.multiple_of(band_row * columns + start, 32), CHUNK)
        grad = stencil(padded, taps_ref, 3 * row if edge else row, start, -1)
        grad = cot_ref[band_row, at, :].astype(jnp.float32) + grad
        density = density_ref[held, :]
        density = jnp.concatenate([density] * (grad.shape[1] // density.shape[1]), axis=1)
        cells_ref[cells, :] = (grad / density).astype(jnp.bfloat16)


def back(edges, grad_edge, grad_mid, taps, cotangent, density):
    lat_rows, columns, width = cotangent.shape
    edge = len(edges) > 0
    rows = 2 if edge else lat_rows - 2
    vmem = pl.BlockSpec(memory_space=pltpu.VMEM)
    depth = 6 if edge else lat_rows
    return pl.pallas_call(
        functools.partial(back_kernel, edge),
        out_shape=jax.ShapeDtypeStruct((rows * columns, width), jnp.bfloat16),
        in_specs=[vmem] * (len(edges) + 5),
        out_specs=vmem,
        scratch_shapes=[pltpu.VMEM((depth, columns + 2 * HALO, width), jnp.bfloat16)],
        cost_estimate=pl.CostEstimate(
            flops=40 * rows * columns * width,
            bytes_accessed=10 * rows * columns * width,
            transcendentals=0,
        ),
        compiler_params=pltpu.CompilerParams(vmem_limit_bytes=36 << 20),
    )(*edges, grad_edge, grad_mid, taps, cotangent, density)


def outer_sum(sums, cells):
    return lax.dot_general(
        sums, cells, (((0,), (0,)), ((), ())), preferred_element_type=jnp.float32
    )


def on_device(
    obs_rows,
    obs_instr,
    obs_target,
    obs_cell,
    embed_weight,
    background,
    stencil_taps,
    weight_in,
    weight_out,
    grid_cotangent,
):
    peer_count = lax.axis_size(("tile", "stream"))
    stream = lax.axis_index("stream")
    swap = [(0, 1), (1, 0)]
    rows_dev, features = obs_rows.shape
    instr_dev = embed_weight.shape[0]
    capacity = 2 * rows_dev // peer_count
    lat_rows, lon_cells, width = grid_cotangent.shape
    band_cells = lat_rows * lon_cells
    other_weight = lax.ppermute(embed_weight, "stream", swap)
    weights = jnp.where(
        stream == 0,
        jnp.concatenate([embed_weight, other_weight], axis=0),
        jnp.concatenate([other_weight, embed_weight], axis=0),
    ).reshape(2 * instr_dev * features, width)
    destination = obs_target[:, 0]
    onehot = (destination[:, None] == jnp.arange(peer_count, dtype=jnp.int32)[None, :]).astype(
        jnp.int32
    )
    running = jnp.cumsum(onehot, axis=0)
    totals = running[-1]
    position = jnp.sum((running - onehot) * onehot, axis=1)
    slot_index = destination * capacity + position
    slot_total = peer_count * capacity
    spare = instr_dev * band_cells
    send_rows, send_codes = pack(
        slot_index, obs_instr * band_cells + obs_cell, obs_rows, slot_total
    )
    send_codes = jnp.where(
        jnp.arange(capacity, dtype=jnp.int32)[None, :] < totals[:, None],
        send_codes.reshape(peer_count, capacity),
        spare,
    )
    code_rows = capacity // features
    padding = -2 * code_rows % 16
    coded = jnp.concatenate(
        [
            (send_codes // 256).reshape(peer_count, code_rows, features),
            (send_codes % 256).reshape(peer_count, code_rows, features),
            jnp.zeros((peer_count, padding, features), jnp.int32),
        ],
        axis=1,
    ).astype(jnp.bfloat16)
    recv_rows = lax.all_to_all(
        jnp.concatenate([send_rows.reshape(peer_count, capacity, features), coded], axis=1),
        ("tile", "stream"),
        split_axis=0,
        concat_axis=0,
        tiled=True,
    )
    pitch = capacity + 2 * code_rows + padding
    digits = recv_rows[:, capacity : capacity + 2 * code_rows].astype(jnp.int32)
    recv_codes = (digits[:, :code_rows] * 256 + digits[:, code_rows:]).reshape(
        peer_count, capacity
    )
    held = jnp.sum((recv_codes < spare).astype(jnp.int32), axis=1)
    bounds = (jnp.max(held.reshape(-1, 2), axis=1) + 7) // 8
    recv_cells = jnp.where(recv_codes < spare, recv_codes % band_cells, band_cells)
    sums, field, density = deposit_cells(
        recv_codes.reshape(slot_total),
        recv_cells.reshape(slot_total),
        bounds,
        recv_rows.reshape(peer_count * pitch, features),
        weights,
        background,
        instr_dev,
        band_cells,
        capacity,
        pitch,
    )
    field = field.reshape(lat_rows, lon_cells, width)
    matrices = (weight_in, weight_out, weight_in.T, weight_out.T)
    edges = edge_rows(field[:1], field[-1:])
    mid_output, mid_grad = layer((), field, stencil_taps, matrices, grid_cotangent)
    edges, mid_grad = lax.optimization_barrier((edges, mid_grad))
    edge_output, edge_grad = layer(edges, field, stencil_taps, matrices, grid_cotangent)
    grad_edges = edge_rows(edge_grad[:1], edge_grad[1:])
    grid_output = jnp.concatenate([edge_output[:1], mid_output, edge_output[1:]], axis=0)
    mid_cells = back((), edge_grad, mid_grad, stencil_taps, grid_cotangent, density)
    local_grad = outer_sum(sums[lon_cells : band_cells - lon_cells], mid_cells)
    edge_cells = back(grad_edges, edge_grad, mid_grad, stencil_taps, grid_cotangent, density)
    local_grad = local_grad + outer_sum(sums[:lon_cells], edge_cells[:lon_cells])
    local_grad = local_grad + outer_sum(sums[band_cells - lon_cells :], edge_cells[lon_cells:])
    tiles = peer_count // 2
    shares = local_grad.astype(jnp.bfloat16).reshape(2, tiles, -1, width)
    shares = lax.all_to_all(
        jnp.swapaxes(shares, 0, 1).reshape(peer_count, -1, width),
        ("tile", "stream"),
        split_axis=0,
        concat_axis=0,
        tiled=True,
    )
    piece = jnp.sum(shares.astype(jnp.float32), axis=0).astype(jnp.bfloat16)
    embed_grad = gathered_over_tile(piece).astype(jnp.float32)
    return (grid_output, embed_grad.reshape(embed_weight.shape))


def solution(mesh):
    in_specs = (
        P(("parts", "tile", "stream"), None),
        P(("parts", "tile", "stream")),
        P(("parts", "tile", "stream"), None),
        P(("parts", "tile", "stream")),
        P("stream", None, None),
        P(),
        P(),
        P(),
        P(),
        P(("parts", "tile", "stream"), None, None),
    )
    out_specs = (P(("parts", "tile", "stream"), None, None), P(("parts", "stream"), None, None))
    return jax.shard_map(
        on_device, mesh=mesh, in_specs=in_specs, out_specs=out_specs, check_vma=False
    )
```
